128 devices in a mesh: grp: 4 (over x), row: 2 (over core), col: 16 (over z, y).
Axes of the slice: x: 4, y: 4, z: 4, core: 2. Of those that a mesh axis runs over, the one named last changes fastest.
Arguments:
- partials: bfloat16 [4, 4, 8192, 8192], P('grp', None, 'row', 'col'), may hold values from -0.2 to 1.6, as said below
- slot_factor: int32 [4], replicated, may hold values from 0 to 3, each once
- previous: float32 [4, 8192, 256], P('grp', 'col'), may hold values from -6 to 6
Outputs:
- bases: float32 [4, 8192, 256], P('grp', ('col', 'row'))
The draws below stay inside these ranges and needn't reach their ends.
Inputs may be any that keep to these rules, and one draw needn't show every extreme that they name: slot_factor names every factor once. Each partials[g, f] is a symmetric matrix.
All inputs are finite; a program needn't handle non-finite values.
Results may differ from the reference program's by a relative error of at most 0.0003.
Values sent between devices are 32-bit elements; how exact they have to be, the bound alone decides.
No kernel may reach another device: no remote copies, remote signals or barrier semaphores. Data moves between devices by JAX's collectives and lax.ppermute only.
A program may use at most 192 MiB of HBM per device.

```python
import math
import jax
import jax.numpy as jnp
from jax import lax

ORDER = 8192
RANK = 256
ITERS = 2
SOURCES = 4
FACTORS = 4


def draw_partials(key, part):
    key = jax.random.fold_in(key, 11)
    factor_keys = jax.random.split(key, SOURCES * FACTORS)

    def draw_one(sub_key):
        noise_key, diag_key = jax.random.split(sub_key)
        raw_noise = jax.random.truncated_normal(noise_key, -6.0, 6.0, (ORDER, ORDER), jnp.float32)
        noise_scale = 0.1
        log_low = math.log(0.1)
        log_high = math.log(1.0)
        symmetric = (raw_noise + raw_noise.T) * (noise_scale / math.sqrt(2.0 * ORDER))
        diagonal = jnp.exp(jax.random.uniform(diag_key, (ORDER,), jnp.float32, log_low, log_high))
        return (symmetric + jnp.diag(diagonal)).astype(jnp.bfloat16)
    return lax.map(draw_one, factor_keys).reshape(SOURCES, FACTORS, ORDER, ORDER)


def block_levels(stream_key, shape, cuts, least, high):
    factor_of = 1.0
    for axis_at, blocks in cuts:
        draws = jax.random.uniform(jax.random.fold_in(jax.random.fold_in(stream_key, 6), axis_at), (blocks,), jnp.float32, least / len(cuts), high / len(cuts))
        factor_of = factor_of * jnp.repeat(jnp.exp(draws), shape[axis_at] // blocks).reshape((-1,) + (1,) * (len(shape) - 1 - axis_at))
    return factor_of


def noise(key, extent, width, reach, cuts=(), held_as=jnp.bfloat16):
    entries = jax.random.normal(key, extent, jnp.float32) * width
    if len(cuts) > 0:
        entries = block_levels(key, extent, cuts, -0.22, 0.18) * entries
    return jnp.clip(entries, min=-reach, max=reach).astype(held_as)


def setup_inputs(seed: int = 0) -> dict:
    key_of = jax.random.split(jax.random.key(seed), 4)
    partials = draw_partials(jax.random.fold_in(key_of[3], 71), 0)
    slot_factor = jax.random.permutation(key_of[1], FACTORS).astype(jnp.int32)
    previous = noise(key_of[2], (FACTORS, ORDER, RANK), 1.0, 6.0, ((0, 4), (1, 16)), jnp.float32)
    return dict(partials=partials, slot_factor=slot_factor, previous=previous)


PRECISE = lax.Precision.HIGHEST

def cholesky_qr(image_rows):
    gram_matrix = jnp.dot(image_rows.T.astype(jnp.float32), image_rows.astype(jnp.float32), precision=PRECISE, preferred_element_type=jnp.float32) / ORDER
    lower_factor = jnp.linalg.cholesky(gram_matrix)
    return jax.scipy.linalg.solve_triangular(lower_factor, image_rows.T, lower=True).T

def refresh(factor, start_basis):
    current = start_basis
    for turn_index in range(ITERS):
        image_rows = jnp.dot(factor.astype(jnp.float32), current.astype(jnp.float32), precision=PRECISE, preferred_element_type=jnp.float32)
        current = cholesky_qr(image_rows)
    return current

def reference(partials, slot_factor, previous):

    def per_slot(slot_index):
        chosen = lax.dynamic_index_in_dim(partials, slot_factor[slot_index], axis=1, keepdims=False)
        factor = chosen[0].astype(jnp.float32)
        for source_index in range(1, SOURCES):
            factor = factor + chosen[source_index].astype(jnp.float32)
        return refresh(factor, previous[slot_index])
    return lax.map(per_slot, jnp.arange(FACTORS, dtype=jnp.int32))
```

```python
import jax
import jax.numpy as jnp
from jax import lax
from jax.experimental import pallas as pl
from jax.experimental.pallas import tpu as pltpu
from jax.sharding import PartitionSpec as P

ORDER = 8192
RANK = 256
PRECISE = lax.Precision.HIGHEST
NAMES = ("grp", "row", "col")
F32 = jnp.float32
VMEM_LIMIT = 48 * 2**20
NO_COST = pl.CostEstimate(flops=0, bytes_accessed=0, transcendentals=0)

MASKS = ((1, 3), (3, 1))
ORDERS = ("xyz", "yzx", "zxy")
WIDTHS = (64, 96, 96)
OFFSETS = (0, 64, 160)
PARTS = range(3)


def hop(value, axis, step):
    pairs = []
    for g in range(4):
        for r in range(2):
            mask = MASKS[r][step]
            for z in range(4):
                for y in range(4):
                    gg = g ^ mask if axis == "x" else g
                    zz = z ^ mask if axis == "z" else z
                    yy = y ^ mask if axis == "y" else y
                    pairs.append(((g * 2 + r) * 16 + z * 4 + y, (gg * 2 + r) * 16 + zz * 4 + yy))
    return lax.ppermute(value, NAMES, pairs)


def swap_core(value):
    return lax.ppermute(value, "row", [(0, 1), (1, 0)])


def precise_dot(left, right, dims):
    return lax.dot_general(
        left, right, (dims, ((), ())), precision=PRECISE, preferred_element_type=F32
    )


def split3(value):
    high = value.astype(jnp.bfloat16)
    rest = value - high.astype(F32)
    mid = rest.astype(jnp.bfloat16)
    low = (rest - mid.astype(F32)).astype(jnp.bfloat16)
    return jnp.concatenate([high, mid, low], axis=0)


def fold3(product):
    n = product.shape[0] // 3
    return product[:n] + (product[n : 2 * n] + product[2 * n :])


class Chain:
    def __init__(self):
        self.token = None

    def call(self, name, body, ins, outs, scratch=()):
        token = [] if self.token is None else [self.token]
        count = len(ins)

        def kernel(*refs):
            mine = refs[:count] + refs[count + len(token) :]
            mine = mine[: count + len(outs)] + mine[count + len(outs) + 1 :]
            refs[count + len(token) + len(outs)][...] = jnp.zeros((8, 128), F32)
            body(*mine)

        vmem = pl.BlockSpec(memory_space=pltpu.VMEM)
        *got, self.token = pl.pallas_call(
            kernel,
            in_specs=[vmem] * count + [pl.BlockSpec(memory_space=pl.ANY)] * len(token),
            out_specs=[vmem] * (len(outs) + 1),
            out_shape=[jax.ShapeDtypeStruct(o, F32) for o in outs]
            + [jax.ShapeDtypeStruct((8, 128), F32)],
            scratch_shapes=list(scratch),
            compiler_params=pltpu.CompilerParams(vmem_limit_bytes=VMEM_LIMIT),
            cost_estimate=NO_COST,
            name=name,
        )(*ins, *token)
        return got


def first_product(table, partials, starts, pair):
    x0 = 2 * pair

    def body(tab, p_low, p_high, x_ref, a_ref, bs_ref, bk_ref, cs_ref, ck_ref, left):
        @pl.when(pl.program_id(1) == 0)
        def _():
            left[...] = split3(x_ref[0])

        for half, p_ref in enumerate((p_low, p_high)):
            for ey in range(4):
                rows = pl.ds(pl.multiple_of(tab[8 + ey] * 256, 256), 256)
                got = fold3(
                    lax.dot_general(
                        left[...],
                        p_ref[0, rows, :],
                        (((1,), (1,)), ((), ())),
                        preferred_element_type=F32,
                    )
                )
                a, b, c = (got[o : o + w] for o, w in zip(OFFSETS, WIDTHS))
                a_ref[0, ey, half, 0] = a
                (bk_ref if ey < 2 else bs_ref)[ey % 2, half, 0, 0] = b
                (cs_ref if half else ck_ref)[0, 0, ey] = c

    wa, wb, wc = WIDTHS
    shapes = [(2, 4, 2, 2, wa, 256)] + [(2, 2, 2, 2, wb, 256)] * 2 + [(2, 2, 4, wc, 256)] * 2
    blocks = [(1, 4, 2, 1, wa, 256)] + [(2, 2, 1, 1, wb, 256)] * 2 + [(1, 1, 4, wc, 256)] * 2
    maps = [
        lambda i, k, tab: (i, 0, 0, k, 0, 0),
        lambda i, k, tab: (0, 0, k, i, 0, 0),
        lambda i, k, tab: (0, 0, k, i, 0, 0),
        lambda i, k, tab: (k, i, 0, 0, 0),
        lambda i, k, tab: (k, i, 0, 0, 0),
    ]
    a, bs, bk, cs, ck = pl.pallas_call(
        body,
        grid_spec=pltpu.PrefetchScalarGridSpec(
            num_scalar_prefetch=1,
            grid=(2, 2),
            in_specs=[
                pl.BlockSpec((1, 1024, 512), lambda i, k, tab: (tab[i + x0], tab[4 + k], 0)),
                pl.BlockSpec((1, 1024, 512), lambda i, k, tab: (tab[i + x0], tab[6 + k], 0)),
                pl.BlockSpec((1, RANK, 512), lambda i, k, tab: (i, 0, 0)),
            ],
            out_specs=[pl.BlockSpec(b, m) for b, m in zip(blocks, maps)],
            scratch_shapes=[pltpu.VMEM((3 * RANK, 512), jnp.bfloat16)],
        ),
        out_shape=[jax.ShapeDtypeStruct(n, F32) for n in shapes],
        compiler_params=pltpu.CompilerParams(vmem_limit_bytes=VMEM_LIMIT),
        cost_estimate=NO_COST,
        name="first_product",
    )(table, partials, partials, starts)
    b_shape = (2, 4, 2, wb, 256)
    return (
        a.reshape(2, 4, 4, wa, 256),
        (bs.reshape(b_shape), bk.reshape(b_shape)),
        (cs, ck),
    )


def second_product(chain, part, half, table, partials, image, before=None):
    rk = WIDTHS[part]
    order = ORDERS[part]
    span = {ax: (0, 1, 2, 3) for ax in "xyz"}
    span[order[0]] = (2, 3) if half else (0, 1)
    x0 = span["x"][0]
    whole = len(span["y"]) == 4
    pieces = [(ez, None) for ez in span["z"]] if whole else [
        (ez, ey) for ez in span["z"] for ey in span["y"]
    ]

    def body(tab, *refs):
        p_refs, v_ref = refs[: len(pieces)], refs[len(pieces)]
        o_ref, token_ref = refs[-2:]
        token_ref[...] = jnp.zeros((8, 128), F32)
        total = None
        for (ez, one), p_ref in zip(pieces, p_refs):
            for ey in span["y"] if one is None else (one,):
                pos = {"x": 0, "y": ey - span["y"][0], "z": ez - span["z"][0]}
                rows = pl.ds(pl.multiple_of(tab[8 + ey] * 256, 256), 256)
                got = jnp.dot(
                    split3(v_ref[tuple(pos[ax] for ax in order)]),
                    p_ref[0, rows, :] if one is None else p_ref[0],
                    preferred_element_type=F32,
                )
                total = got if total is None else total + got
        total = fold3(total)
        first = tab[12] == 0
        for e in range(2):
            mine = jnp.where(first, total[:, e * 256 : e * 256 + 256], total[:, 256 - e * 256 :][:, :256])
            o_ref[e, 0] = mine if before is None else mine + refs[len(pieces) + 1][e, 0]

    def in_map(i, tab):
        return tuple(i if ax == "x" else 0 for ax in order) + (0, 0)

    def rows(ez, ey):
        if ey is None:
            return lambda i, tab: (tab[i + x0], tab[4 + ez], 0)
        return lambda i, tab: (tab[i + x0], tab[4 + ez] * 4 + tab[8 + ey], 0)

    out_spec = pl.BlockSpec((2, 1, rk, 256), lambda i, tab: (0, i, 0, 0))
    operands = [table] + [partials] * len(pieces) + [image]
    in_specs = [pl.BlockSpec((1, 1024 if whole else 256, 512), rows(*p)) for p in pieces]
    block = tuple(1 if ax == "x" else len(span[ax]) for ax in order)
    in_specs.append(pl.BlockSpec(block + (rk, 256), in_map))
    if before is not None:
        operands.append(before)
        in_specs.append(out_spec)
    operands.append(chain.token)
    in_specs.append(pl.BlockSpec(memory_space=pl.ANY))
    nx = len(span["x"])
    out, chain.token = pl.pallas_call(
        body,
        grid_spec=pltpu.PrefetchScalarGridSpec(
            num_scalar_prefetch=1,
            grid=(nx,),
            in_specs=in_specs,
            out_specs=[out_spec, pl.BlockSpec((8, 128), lambda i, tab: (0, 0))],
        ),
        out_shape=[
            jax.ShapeDtypeStruct((2, nx, rk, 256), F32),
            jax.ShapeDtypeStruct((8, 128), F32),
        ],
        compiler_params=pltpu.CompilerParams(vmem_limit_bytes=VMEM_LIMIT),
        cost_estimate=NO_COST,
        name="second_product",
    )(*operands)
    return out


def add_halves(chain, keeps, gots, axis):
    shape = list(keeps[0].shape)
    shape[axis] = 2
    shape[2] *= len(keeps) if axis == 1 else 1
    count = len(keeps)

    def body(*refs):
        upper, lower = refs[-2:]
        width = lower.shape[2] // count
        for h in range(count):
            for n, out in enumerate((lower, upper)):
                at = [slice(None)] * 5
                at[axis] = slice(2 * n, 2 * n + 2)
                to = [slice(None)] * 5
                if count > 1:
                    to[2] = slice(h * width, h * width + width)
                out[tuple(to)] = refs[h][tuple(at)] + refs[count + h][tuple(at)]

    return chain.call("add_halves", body, [*keeps, *gots], [tuple(shape)] * 2)


def add_whole(chain, keep, got):
    def body(k_ref, g_ref, out):
        out[...] = k_ref[...] + g_ref[...]

    return chain.call("add_whole", body, [keep, got], [keep.shape])[0]


def add_flipped(chain, keep, got, axis):
    def body(k_ref, g_ref, out):
        for n in range(2):
            at = [slice(None)] * 5
            to = [slice(None)] * 5
            at[axis], to[axis] = slice(1 - n, 2 - n), slice(n, n + 1)
            out[tuple(to)] = k_ref[tuple(to)] + g_ref[tuple(at)]

    return chain.call("add_flipped", body, [keep, got], [keep.shape])[0]


def join(chain, low, high, axis):
    shape = list(low.shape)
    shape[axis] = 4

    def body(l_ref, h_ref, out):
        for n, ref in enumerate((l_ref, h_ref)):
            at = [slice(None)] * 5
            at[axis] = slice(2 * n, 2 * n + 2)
            out[tuple(at)] = ref[...]

    return chain.call("join", body, [low, high], [tuple(shape)])[0]


def image_sum(chain, first, second):
    (a0, b0, c0), (a1, b1, c1) = first, second
    got_b0, got_c0 = hop(b0[0], "y", 0), hop(c0[0], "z", 0)
    got_a = hop(a1, "x", 0)
    got_b1, got_c1 = hop(b1[0], "y", 0), hop(c1[0], "z", 0)
    keeps = [None] * 3
    gots = [None] * 3
    upper, keeps[0] = add_halves(chain, [a0], [got_a], 1)
    gots[0] = hop(upper, "y", 0)
    upper, keeps[1] = add_halves(chain, [b0[1], b1[1]], [got_b0, got_b1], 1)
    gots[1] = hop(upper, "z", 0)
    upper = add_whole(chain, c1[1], got_c1)
    gots[2] = hop(upper, "x", 0)
    keeps[2] = add_whole(chain, c0[1], got_c0)
    nexts = []
    for p in PARTS:
        upper, keeps[p] = add_halves(chain, [keeps[p]], [gots[p]], 2)
        nexts.append(hop(upper, ORDERS[p][2], 0))
    gots = nexts
    sums = [None] * 3
    for axis in (-1, 0, 1, 2):
        nexts = []
        for p in PARTS:
            if axis < 0:
                sums[p] = add_whole(chain, keeps[p], gots[p])
            else:
                sums[p] = add_flipped(chain, sums[p], gots[p], axis)
            if axis < 2:
                nexts.append(hop(sums[p], ORDERS[p][axis + 1], 1))
        gots = nexts
    return sums


def own_gram(chain, sums):
    def body(a_ref, b_ref, c_ref, out, image):
        for ref, o, w in zip((a_ref, b_ref, c_ref), OFFSETS, WIDTHS):
            image[o : o + w, :] = ref[0, 0, 0]
        out[...] = precise_dot(image[...], image[...], ((1,), (1,))) / ORDER

    return chain.call(
        "own_gram", body, sums, [(RANK, RANK)], [pltpu.VMEM((RANK, RANK), F32)]
    )[0]


def normal_gram(chain, inverse, product):
    def body(i_ref, p_ref, image, gram):
        image[...] = precise_dot(i_ref[...], p_ref[...], ((1,), (0,)))
        gram[...] = precise_dot(image[...], image[...], ((1,), (1,))) / ORDER

    return chain.call(
        "normal_gram", body, [inverse, product], [(RANK, RANK)] * 2
    )


class GramSum:
    steps = (("y", 0), ("y", 1), ("z", 0), ("z", 1))

    def __init__(self, gram):
        self.core = lax.axis_index("row")
        half = RANK // 2
        self.mine = lax.dynamic_slice_in_dim(gram, self.core * half, half, 0)
        other = lax.dynamic_slice_in_dim(gram, (1 - self.core) * half, half, 0)
        self.got = swap_core(other)

    def step(self, chain, n):
        self.mine = add_whole(chain, self.mine, self.got)
        if n < 4:
            self.got = hop(self.mine, *self.steps[n])
        else:
            self.got = swap_core(self.mine)

    def total(self):
        low = jnp.where(self.core == 0, self.mine, self.got)
        high = jnp.where(self.core == 0, self.got, self.mine)
        return jnp.concatenate([low, high], axis=0)


BLOCK = 64


def block_inverse(block):
    row = lax.broadcasted_iota(jnp.int32, (BLOCK, 128), 0)
    col = lax.broadcasted_iota(jnp.int32, (BLOCK, 128), 1)
    both = jnp.concatenate([block, jnp.zeros((BLOCK, 128 - BLOCK), F32)], axis=1)
    both = jnp.where(col == row + BLOCK, 1.0, both)
    for s in range(0, BLOCK, 8):
        cols = [jnp.broadcast_to(both[:, s + j : s + j + 1], (BLOCK, 128)) for j in range(8)]
        for k in range(8):
            at = s + k
            scale = lax.rsqrt(jnp.broadcast_to(cols[k][at : at + 1, :], (8, 128)))[:1]
            pivot = both[at : at + 1, :] * scale
            below = jnp.where(row > at, cols[k] * scale, 0.0)
            for j in range(k + 1, 8):
                cols[j] = cols[j] - below * (cols[j][at : at + 1, :] * scale)
            both = jnp.where(row == at, pivot, both - below * pivot)
    return both[:, BLOCK:]


def eliminate(gram, inverse, work):
    row = lax.broadcasted_iota(jnp.int32, (RANK, RANK), 0)
    col = lax.broadcasted_iota(jnp.int32, (RANK, RANK), 1)
    work[:, :RANK] = gram[...]
    work[:, RANK:] = (row == col).astype(F32)
    for at in range(0, RANK, BLOCK):
        rows = slice(at, at + BLOCK)
        low = at // 128 * 128
        high = RANK + (at + BLOCK + 127) // 128 * 128
        upper = precise_dot(block_inverse(work[rows, rows]), work[rows, low:high], ((1,), (0,)))
        inverse[rows, : high - RANK] = upper[:, RANK - low :]
        if high < 2 * RANK:
            inverse[rows, high - RANK :] = jnp.zeros((BLOCK, 2 * RANK - high), F32)
        if at + BLOCK < RANK:
            left = upper[:, at + BLOCK - low : RANK - low]
            work[at + BLOCK :, low:high] -= precise_dot(left, upper, ((0,), (0,)))


def lower_inverse(chain, gram):
    return chain.call(
        "lower_inverse",
        eliminate,
        [gram],
        [(RANK, RANK)],
        [pltpu.VMEM((RANK, 2 * RANK), F32)],
    )[0]


def normalise(chain, gram, image):
    def body(g_ref, i_ref, out, inverse, work):
        eliminate(g_ref, inverse, work)
        out[0] = precise_dot(i_ref[...], inverse[...], ((0,), (1,)))

    return chain.call(
        "normalise",
        body,
        [gram, image],
        [(1, 256, RANK)],
        [pltpu.VMEM((RANK, RANK), F32), pltpu.VMEM((RANK, 2 * RANK), F32)],
    )[0]


def on_device(partials, slot_factor, previous):
    partials = partials[0]
    core = lax.axis_index("row")
    grp = lax.axis_index("grp")
    col = lax.axis_index("col")
    masks = jnp.where(
        core == 0, jnp.array([0, 3, 1, 2], jnp.int32), jnp.array([0, 1, 3, 2], jnp.int32)
    )
    table = jnp.concatenate(
        [
            slot_factor[grp ^ masks],
            (col // 4) ^ masks,
            (col % 4) ^ masks,
            jnp.stack([core, 1 - core]).astype(jnp.int32),
        ]
    )
    start = previous[0].T
    pair = jnp.stack([start, hop(start, "x", 1)])
    other = hop(pair, "x", 0)

    chain = Chain()
    first = first_product(table, partials, pair, 0)
    second = first_product(table, partials, other, 1)
    held = image_sum(chain, first, second)

    gots = [hop(held[p], ORDERS[p][2], 0) for p in PARTS]
    gram = GramSum(own_gram(chain, held))
    for axis in (2, 1):
        nexts = []
        for p in PARTS:
            held[p] = join(chain, held[p], gots[p], axis)
            nexts.append(hop(held[p], ORDERS[p][axis - 1], 0))
        gots = nexts
        gram.step(chain, 2 - axis)
    early = []
    for p in PARTS:
        early.append(second_product(chain, p, False, table, partials, held[p]))
        gram.step(chain, 2 + p)
    late = [
        second_product(chain, p, True, table, partials, gots[p], None if p == 0 else early[p])
        for p in PARTS
    ]
    slots = [jnp.concatenate([early[0], late[0]], axis=1), late[1], late[2]]
    both = jnp.concatenate(slots, axis=2)
    other = swap_core(both[1])
    inverse = lower_inverse(chain, gram.total())
    mine = both[0] + jnp.stack([other[0], other[2], other[1], other[3]])
    mine = mine[:2] + hop(mine[2:], "x", 0)
    product = mine[0] + hop(mine[1], "x", 1)

    image, gram = normal_gram(chain, inverse, product)
    gram = GramSum(gram)
    for n in range(5):
        gram.step(chain, n)
    return normalise(chain, gram.total(), image)


def solution(mesh):
    return jax.shard_map(
        on_device,
        mesh=mesh,
        in_specs=(P("grp", None, "row", "col"), P(), P("grp", "col", None)),
        out_specs=P("grp", ("col", "row"), None),
        check_vma=False,
    )
```

```python
import functools

import jax
import jax.numpy as jnp
from jax import lax
from jax.experimental import pallas as pl
from jax.experimental.pallas import tpu as pltpu
from jax.sharding import PartitionSpec as P

ORDER = 8192
RANK = 256
PRECISE = lax.Precision.HIGHEST
NAMES = ("grp", "row", "col")
F32 = jnp.float32
VMEM_LIMIT = 16 * 2**20


def costs(size):
    return pl.CostEstimate(flops=size * 2**30, bytes_accessed=0, transcendentals=0)

MASKS = ((1, 3, 2), (3, 1, 2))
ORDERS = ("xyz", "yzx", "zxy")
WIDTHS = (64, 96, 96)
OFFSETS = (0, 64, 160)


def hop(value, axis, step):
    pairs = []
    for g in range(4):
        for r in range(2):
            mask = MASKS[r][step]
            for z in range(4):
                for y in range(4):
                    gg = g ^ mask if axis == "x" else g
                    zz = z ^ mask if axis == "z" else z
                    yy = y ^ mask if axis == "y" else y
                    pairs.append(((g * 2 + r) * 16 + z * 4 + y, (gg * 2 + r) * 16 + zz * 4 + yy))
    return lax.ppermute(value, NAMES, pairs)


def swap_core(value):
    return lax.ppermute(value, "row", [(0, 1), (1, 0)])


def precise_dot(left, right, dims):
    return lax.dot_general(
        left, right, (dims, ((), ())), precision=PRECISE, preferred_element_type=F32
    )


def split3(value):
    high = value.astype(jnp.bfloat16)
    rest = value - high.astype(F32)
    mid = rest.astype(jnp.bfloat16)
    low = (rest - mid.astype(F32)).astype(jnp.bfloat16)
    return jnp.concatenate([high, mid, low], axis=0)


def fold3(product):
    n = product.shape[0] // 3
    return product[:n] + (product[n : 2 * n] + product[2 * n :])


class Chain:
    def __init__(self):
        self.token = None

    def call(self, name, body, ins, outs, scratch=(), cost=1):
        token = [] if self.token is None else [self.token]
        count = len(ins)

        def kernel(*refs):
            mine = refs[:count] + refs[count + len(token) :]
            mine = mine[: count + len(outs)] + mine[count + len(outs) + 1 :]
            refs[count + len(token) + len(outs)][...] = jnp.zeros((8, 128), F32)
            body(*mine)

        vmem = pl.BlockSpec(memory_space=pltpu.VMEM)
        *got, self.token = pl.pallas_call(
            kernel,
            in_specs=[vmem] * count + [pl.BlockSpec(memory_space=pl.ANY)] * len(token),
            out_specs=[vmem] * (len(outs) + 1),
            out_shape=[jax.ShapeDtypeStruct(o, F32) for o in outs]
            + [jax.ShapeDtypeStruct((8, 128), F32)],
            scratch_shapes=list(scratch),
            compiler_params=pltpu.CompilerParams(vmem_limit_bytes=VMEM_LIMIT),
            cost_estimate=costs(cost),
            name=name,
        )(*ins, *token)
        return got


def load(partials):
    def body(source, target, sem):
        copy = pltpu.make_async_copy(source, target, sem)
        copy.start()
        copy.wait()

    return pl.pallas_call(
        body,
        in_specs=[pl.BlockSpec(memory_space=pltpu.HBM)],
        out_specs=pl.BlockSpec(memory_space=pltpu.VMEM),
        out_shape=jax.ShapeDtypeStruct(partials.shape, partials.dtype),
        scratch_shapes=[pltpu.SemaphoreType.DMA],
        compiler_params=pltpu.CompilerParams(vmem_limit_bytes=VMEM_LIMIT),
        cost_estimate=pl.CostEstimate(flops=4 * 2**30, bytes_accessed=0, transcendentals=0),
        name="load",
    )(partials)


def first_product(table, partials, starts, pair, after=None):
    x0 = 2 * pair

    def body(tab, p_low, p_high, x_ref, *rest):
        a_ref, bs_ref, bk_ref, cs_ref, ck_ref, left = rest[-6:]

        @pl.when(pl.program_id(1) == 0)
        def _():
            left[...] = split3(x_ref[0])

        for half, p_ref in enumerate((p_low, p_high)):
            for ey in range(4):
                rows = pl.ds(pl.multiple_of(tab[8 + ey] * 256, 256), 256)
                got = fold3(
                    lax.dot_general(
                        left[...],
                        p_ref[0, rows, :],
                        (((1,), (1,)), ((), ())),
                        preferred_element_type=F32,
                    )
                )
                a, b, c = (got[o : o + w] for o, w in zip(OFFSETS, WIDTHS))
                a_ref[0, ey, half, 0] = a
                (bk_ref if ey < 2 else bs_ref)[ey % 2, half, 0, 0] = b
                (cs_ref if half else ck_ref)[0, 0, ey] = c

    wa, wb, wc = WIDTHS
    shapes = [(2, 4, 2, 2, wa, 256)] + [(2, 2, 2, 2, wb, 256)] * 2 + [(2, 2, 4, wc, 256)] * 2
    blocks = [(1, 4, 2, 1, wa, 256)] + [(2, 2, 1, 1, wb, 256)] * 2 + [(1, 1, 4, wc, 256)] * 2
    maps = [
        lambda i, k, tab: (i, 0, 0, k, 0, 0),
        lambda i, k, tab: (0, 0, k, i, 0, 0),
        lambda i, k, tab: (0, 0, k, i, 0, 0),
        lambda i, k, tab: (k, i, 0, 0, 0),
        lambda i, k, tab: (k, i, 0, 0, 0),
    ]
    a, bs, bk, cs, ck = pl.pallas_call(
        body,
        grid_spec=pltpu.PrefetchScalarGridSpec(
            num_scalar_prefetch=1,
            grid=(2, 2),
            in_specs=[
                pl.BlockSpec((1, 1024, 512), lambda i, k, tab: (tab[i + x0], tab[4 + k], 0)),
                pl.BlockSpec((1, 1024, 512), lambda i, k, tab: (tab[i + x0], tab[6 + k], 0)),
                pl.BlockSpec((1, RANK, 512), lambda i, k, tab: (i, 0, 0)),
            ]
            + [pl.BlockSpec(memory_space=pl.ANY)] * (after is not None),
            out_specs=[pl.BlockSpec(b, m) for b, m in zip(blocks, maps)],
            scratch_shapes=[pltpu.VMEM((3 * RANK, 512), jnp.bfloat16)],
        ),
        out_shape=[jax.ShapeDtypeStruct(n, F32) for n in shapes],
        compiler_params=pltpu.CompilerParams(vmem_limit_bytes=VMEM_LIMIT),
        cost_estimate=pl.CostEstimate(
            flops=12 * 2**30, bytes_accessed=2**24, transcendentals=0
        ),
        name="first_product",
    )(table, partials, partials, starts, *([] if after is None else [after]))
    b_shape = (2, 4, 2, wb, 256)
    return (
        a.reshape(2, 4, 4, wa, 256),
        (bs.reshape(b_shape), bk.reshape(b_shape)),
        (cs, ck),
    )


def second_product(chain, pieces, table, partials, before=None, last=False):
    every = range(4)
    count = 2 + len(pieces) + (before is not None)

    def body(tab, p_ref, *refs):
        images = refs[: len(pieces)]
        outs = refs[count - 1 :]
        total = outs[-1]
        outs[0][...] = jnp.zeros((8, 128), F32)
        if before is None:
            total[...] = jnp.zeros((4, RANK, 512), F32)
        else:
            total[...] = refs[len(pieces)][...]

        def cell(x, z, y):
            row = pl.multiple_of(tab[4 + z] * 1024 + tab[8 + y] * 256, 256)
            return p_ref[tab[x], pl.ds(row, 256), :]

        def add(x, part, terms):
            got = None
            for v, p in terms:
                term = jnp.dot(split3(v), p, preferred_element_type=F32)
                got = term if got is None else got + term
            rows = slice(OFFSETS[part], OFFSETS[part] + WIDTHS[part])
            total[x, rows, :] += fold3(got)

        for (part, (half, start, size), _), v in zip(pieces, images):
            first = 2 * half

            @pl.loop(0, 4 if part == 1 else 2 if part == 0 else size)
            def _(n, part=part, first=first, start=start, size=size, v=v):
                if part == 0:
                    x = first + n
                    cells = [(v[n, k, z], (x, z, start + k)) for k in range(size) for z in every]
                elif part == 1:
                    x = n
                    cells = [
                        (v[j, k, n], (x, start + k, first + j)) for j in range(2) for k in range(size)
                    ]
                else:
                    x = start + n
                    cells = [(v[j, n, y], (x, first + j, y)) for j in range(2) for y in every]
                add(x, part, [(rows, cell(*c)) for rows, c in cells])

        if last:
            first = tab[12] == 0
            for x in every:
                left, right = total[x, :, :256], total[x, :, 256:]
                outs[2][x] = jnp.where(first, left, right)
                outs[3][(0, 2, 1, 3)[x]] = jnp.where(first, right, left)

    vmem = pl.BlockSpec(memory_space=pltpu.VMEM)
    operands = [partials] + [rows for _, _, rows in pieces]
    operands += ([] if before is None else [before]) + [chain.token]
    shapes = [(4, RANK, 256)] * 2 if last else [(4, RANK, 512)]
    chain.token, partials, *got = pl.pallas_call(
        body,
        in_specs=[pl.BlockSpec(memory_space=pltpu.SMEM)]
        + [vmem] * (len(operands) - 1)
        + [pl.BlockSpec(memory_space=pl.ANY)],
        out_specs=[vmem] * (2 + len(shapes)),
        out_shape=[
            jax.ShapeDtypeStruct((8, 128), F32),
            jax.ShapeDtypeStruct(partials.shape, partials.dtype),
        ]
        + [jax.ShapeDtypeStruct(n, F32) for n in shapes],
        scratch_shapes=[pltpu.VMEM((4, RANK, 512), F32)] if last else [],
        input_output_aliases={1: 1},
        compiler_params=pltpu.CompilerParams(vmem_limit_bytes=VMEM_LIMIT),
        cost_estimate=costs(0),
        name="second_product",
    )(table, *operands)
    return partials, got


def at_half(axis, half):
    index = [slice(None)] * 5
    index[axis] = slice(2 * half, 2 * half + 2)
    return tuple(index)


def add_all(chain, jobs, cost=1):
    outs = []
    for keep, _, axis in jobs:
        shape = list(keep.shape)
        if axis is not None:
            shape[axis] = 2
        outs += [tuple(shape)] * (1 if axis is None else 2)

    def body(*refs):
        n = 2 * len(jobs)
        for j, (_, _, axis) in enumerate(jobs):
            k_ref, g_ref = refs[2 * j], refs[2 * j + 1]
            if axis is None:
                refs[n][...] = k_ref[...] + g_ref[...]
                n += 1
            else:
                for half, out in ((1, refs[n]), (0, refs[n + 1])):
                    out[...] = k_ref[at_half(axis, half)] + g_ref[at_half(axis, half)]
                n += 2

    return chain.call("add_all", body, [v for k, g, _ in jobs for v in (k, g)], outs, (), cost)


def add_whole(chain, keep, got):
    return add_all(chain, [(keep, got, None)])[0]


def add_four(chain, keep, gots):
    def body(k_ref, a_ref, b_ref, c_ref, out):
        out[...] = (k_ref[...] + a_ref[...]) + (b_ref[...] + c_ref[...])

    return chain.call("add_four", body, [keep, *gots], [keep.shape])[0]


def add_flipped(chain, keeps, gots, axis):
    def body(*refs):
        for k_ref, g_ref, out in zip(refs[:3], refs[3:6], refs[6:]):
            for n in range(2):
                at = [slice(None)] * 5
                to = [slice(None)] * 5
                at[axis], to[axis] = slice(1 - n, 2 - n), slice(n, n + 1)
                out[tuple(to)] = k_ref[tuple(to)] + g_ref[tuple(at)]

    return chain.call("add_flipped", body, [*keeps, *gots], [v.shape for v in keeps])


def join(chain, pairs, axis):
    outs = []
    for pair in pairs:
        shape = list(pair[0].shape)
        shape[axis] *= len(pair)
        outs.append(tuple(shape))

    def body(*refs):
        n = 0
        for pair, out in zip(pairs, refs[-len(pairs) :]):
            if len(pair) == 1:
                out[...] = refs[n][...]
            else:
                for half in range(2):
                    out[at_half(axis, half)] = refs[n + half][...]
            n += len(pair)

    return chain.call("join", body, [v for pair in pairs for v in pair], outs)


def image_sum(chain, first, second):
    (a0, b0, c0), (a1, b1, c1) = first, second
    got_b0, got_c0 = hop(b0[0], "y", 0), hop(c0[0], "z", 0)
    got_b1, got_c1, got_a = hop(b1[0], "y", 0), hop(c1[0], "z", 0), hop(a1, "x", 0)
    up_b0, low_b0, low_c = add_all(chain, [(b0[1], got_b0, 1), (c0[1], got_c0, None)], 16)
    up_b1, low_b1, up_c, up_a, low_a = add_all(
        chain, [(b1[1], got_b1, 1), (c1[1], got_c1, None), (a0, got_a, 1)]
    )
    got_b0, got_b1 = hop(up_b0, "z", 0), hop(up_b1, "z", 0)
    got_c, got_a = hop(up_c, "x", 0), hop(up_a, "y", 0)
    low_b, up_b, up_c, low_c, up_a, low_a = add_all(
        chain, [(low_b0, got_b0, None), (low_b1, got_b1, None), (low_c, got_c, 2), (low_a, got_a, 2)]
    )
    keeps = [low_a, low_b, low_c]
    gots = [hop(up_a, "z", 0), hop(up_b, "x", 0), hop(up_c, "y", 0)]
    sums = add_all(chain, [(k, g, None) for k, g in zip(keeps, gots)])
    for axis in range(3):
        gots = [hop(v, o[axis], 1) for v, o in zip(sums, ORDERS)]
        sums = add_flipped(chain, sums, gots, axis)
    return sums


def gram_of(chain, blocks, images, before=None):
    arrays = [v for image in images for v in image]

    def body(*refs):
        out, image = refs[-2:]
        total = None if before is None else refs[len(arrays)][...]
        for z, y in blocks:
            pos = {"x": 0, "y": y, "z": z}
            for p in range(3):
                first, second, third = (pos[ax] for ax in ORDERS[p])
                ref = refs[3 * (2 * (first // 2) + second // 2) + p]
                rows = slice(OFFSETS[p], OFFSETS[p] + WIDTHS[p])
                image[rows, :] = ref[first % 2, second % 2, third]
            got = precise_dot(image[...], image[...], ((1,), (1,))) / ORDER
            total = got if total is None else total + got
        out[...] = total

    return chain.call(
        "gram_of",
        body,
        arrays + ([] if before is None else [before]),
        [(RANK, RANK)],
        [pltpu.VMEM((RANK, RANK), F32)],
    )[0]


def normal_gram(chain, inverse, product):
    def body(i_ref, p_ref, image, gram):
        image[...] = precise_dot(i_ref[...], p_ref[...], ((1,), (0,)))
        gram[...] = precise_dot(image[...], image[...], ((1,), (1,))) / ORDER

    return chain.call(
        "normal_gram", body, [inverse, product], [(RANK, RANK)] * 2
    )


def sum_gram(chain, gram):
    core = lax.axis_index("row")
    half = RANK // 2
    mine = lax.dynamic_slice_in_dim(gram, core * half, half, 0)
    other = lax.dynamic_slice_in_dim(gram, (1 - core) * half, half, 0)
    mine = add_whole(chain, mine, swap_core(other))
    for axis in "yz":
        mine = add_four(chain, mine, [hop(mine, axis, step) for step in range(3)])
    other = swap_core(mine)
    low = jnp.where(core == 0, mine, other)
    high = jnp.where(core == 0, other, mine)
    return jnp.concatenate([low, high], axis=0)


BLOCK = 64


def block_inverse(block):
    row = lax.broadcasted_iota(jnp.int32, (BLOCK, 128), 0)
    col = lax.broadcasted_iota(jnp.int32, (BLOCK, 128), 1)
    both = jnp.concatenate([block, jnp.zeros((BLOCK, 128 - BLOCK), F32)], axis=1)
    both = jnp.where(col == row + BLOCK, 1.0, both)
    for s in range(0, BLOCK, 8):
        cols = [jnp.broadcast_to(both[:, s + j : s + j + 1], (BLOCK, 128)) for j in range(8)]
        for k in range(8):
            at = s + k
            scale = lax.rsqrt(jnp.broadcast_to(cols[k][at : at + 1, :], (8, 128)))[:1]
            pivot = both[at : at + 1, :] * scale
            below = jnp.where(row > at, cols[k] * scale, 0.0)
            for j in range(k + 1, 8):
                cols[j] = cols[j] - below * (cols[j][at : at + 1, :] * scale)
            both = jnp.where(row == at, pivot, both - below * pivot)
    return both[:, BLOCK:]


def eliminate(gram, inverse, work):
    row = lax.broadcasted_iota(jnp.int32, (RANK, RANK), 0)
    col = lax.broadcasted_iota(jnp.int32, (RANK, RANK), 1)
    work[:, :RANK] = gram[...]
    work[:, RANK:] = (row == col).astype(F32)
    for at in range(0, RANK, BLOCK):
        rows = slice(at, at + BLOCK)
        low = at // 128 * 128
        high = RANK + (at + BLOCK + 127) // 128 * 128
        upper = precise_dot(block_inverse(work[rows, rows]), work[rows, low:high], ((1,), (0,)))
        inverse[rows, : high - RANK] = upper[:, RANK - low :]
        if high < 2 * RANK:
            inverse[rows, high - RANK :] = jnp.zeros((BLOCK, 2 * RANK - high), F32)
        if at + BLOCK < RANK:
            left = upper[:, at + BLOCK - low : RANK - low]
            work[at + BLOCK :, low:high] -= precise_dot(left, upper, ((0,), (0,)))


def lower_inverse(chain, gram):
    return chain.call(
        "lower_inverse",
        eliminate,
        [gram],
        [(RANK, RANK)],
        [pltpu.VMEM((RANK, 2 * RANK), F32)],
    )[0]


def normalise(chain, gram, image):
    def body(g_ref, i_ref, out, inverse, work):
        eliminate(g_ref, inverse, work)
        out[0] = precise_dot(i_ref[...], inverse[...], ((0,), (1,)))

    return chain.call(
        "normalise",
        body,
        [gram, image],
        [(1, 256, RANK)],
        [pltpu.VMEM((RANK, RANK), F32), pltpu.VMEM((RANK, 2 * RANK), F32)],
    )[0]


def on_device(partials, slot_factor, previous):
    partials = load(partials[0])
    core = lax.axis_index("row")
    grp = lax.axis_index("grp")
    col = lax.axis_index("col")
    masks = jnp.where(
        core == 0, jnp.array([0, 3, 1, 2], jnp.int32), jnp.array([0, 1, 3, 2], jnp.int32)
    )
    table = jnp.concatenate(
        [
            slot_factor[grp ^ masks],
            (col // 4) ^ masks,
            (col % 4) ^ masks,
            jnp.stack([core, 1 - core]).astype(jnp.int32),
        ]
    )
    start = previous[0].T
    pair = jnp.stack([start, hop(start, "x", 1)])
    other = hop(pair, "x", 0)

    chain = Chain()
    first = first_product(table, partials, pair, 0)
    second = first_product(table, partials, other, 1, first[0])
    held = image_sum(chain, first, second)

    gots = [hop(v, o[2], 0) for v, o in zip(held, ORDERS)]
    low, high = (0, 1), (2, 3)
    gram = gram_of(chain, [(z, y) for z in low for y in low], [held])
    held = join(chain, list(zip(held, gots)), 2)
    beside = [hop(v, o[1], 0) for v, o in zip(held, ORDERS)]
    far_b, far_c = hop(held[1], "y", 0), hop(held[2], "z", 0)

    near = (0, 0, 2)
    product = functools.partial(second_product, chain, table=table)
    partials, total = product(list(zip(range(3), [near] * 3, held)), partials=partials)
    whole_a, beside_b, beside_c = join(
        chain, [(held[0], beside[0]), (beside[1],), (beside[2],)], 1
    )
    far_a = hop(whole_a, "x", 0)
    far_beside_b, far_beside_c = hop(beside_b, "y", 0), hop(beside_c, "z", 0)
    pieces = [(0, (0, 2, 2), beside[0]), (1, (0, 2, 2), beside_b), (2, (0, 2, 2), beside_c)]
    partials, total = product(pieces, partials=partials, before=total[0])
    pieces = [(1, (1, 0, 2), far_b), (2, (1, 0, 2), far_c)]
    partials, total = product(pieces, partials=partials, before=total[0])
    blocks = [(z, y) for z in high for y in low] + [(z, y) for z in low for y in high]
    beside = [beside[0], beside_b, beside_c]
    gram = gram_of(chain, blocks, [held, beside, [held[0], far_b, far_c]], gram)
    pieces = [(0, (1, 0, 4), far_a), (1, (1, 2, 2), far_beside_b), (2, (1, 2, 2), far_beside_c)]
    _, (mine, other_mine) = product(pieces, partials=partials, before=total[0], last=True)
    blocks = [(z, y) for z in high for y in high]
    far = [held[0], far_b, far_c]
    gram = gram_of(chain, blocks, [held, beside, far, [held[0], far_beside_b, far_c]], gram)
    gram = add_whole(chain, gram, swap_core(gram))
    inverse = lower_inverse(chain, gram)
    mine = mine + swap_core(other_mine)
    mine = mine[:2] + hop(mine[2:], "x", 0)
    product = mine[0] + hop(mine[1], "x", 1)

    image, gram = normal_gram(chain, inverse, product)
    return normalise(chain, sum_gram(chain, gram), image)


def solution(mesh):
    return jax.shard_map(
        on_device,
        mesh=mesh,
        in_specs=(P("grp", None, "row", "col"), P(), P("grp", "col", None)),
        out_specs=P("grp", ("col", "row"), None),
        check_vma=False,
    )
```

```python
import functools

import jax
import jax.numpy as jnp
from jax import lax
from jax.experimental import pallas as pl
from jax.experimental.pallas import tpu as pltpu
from jax.sharding import PartitionSpec as P

ORDER = 8192
RANK = 256
PRECISE = lax.Precision.HIGHEST
NAMES = ("grp", "row", "col")
F32 = jnp.float32
VMEM_LIMIT = 16 * 2**20


def costs(size):
    return pl.CostEstimate(flops=size * 2**30, bytes_accessed=0, transcendentals=0)

MASKS = ((1, 3, 2), (3, 1, 2))
ORDERS = ("xyz", "yzx", "zxy")
WIDTHS = (64, 96, 96)
OFFSETS = (0, 64, 160)


def hop(value, axis, step):
    pairs = []
    for g in range(4):
        for r in range(2):
            mask = MASKS[r][step]
            for z in range(4):
                for y in range(4):
                    gg = g ^ mask if axis == "x" else g
                    zz = z ^ mask if axis == "z" else z
                    yy = y ^ mask if axis == "y" else y
                    pairs.append(((g * 2 + r) * 16 + z * 4 + y, (gg * 2 + r) * 16 + zz * 4 + yy))
    return lax.ppermute(value, NAMES, pairs)


def swap_core(value):
    return lax.ppermute(value, "row", [(0, 1), (1, 0)])


def precise_dot(left, right, dims):
    return lax.dot_general(
        left, right, (dims, ((), ())), precision=PRECISE, preferred_element_type=F32
    )


def split3(value):
    high = value.astype(jnp.bfloat16)
    rest = value - high.astype(F32)
    mid = rest.astype(jnp.bfloat16)
    low = (rest - mid.astype(F32)).astype(jnp.bfloat16)
    return jnp.concatenate([high, mid, low], axis=0)


def fold3(product):
    n = product.shape[0] // 3
    return product[:n] + (product[n : 2 * n] + product[2 * n :])


class Chain:
    def __init__(self):
        self.token = None

    def call(self, name, body, ins, outs, scratch=(), cost=1):
        token = [] if self.token is None else [self.token]
        count = len(ins)

        def kernel(*refs):
            mine = refs[:count] + refs[count + len(token) :]
            mine = mine[: count + len(outs)] + mine[count + len(outs) + 1 :]
            refs[count + len(token) + len(outs)][...] = jnp.zeros((8, 128), F32)
            body(*mine)

        vmem = pl.BlockSpec(memory_space=pltpu.VMEM)
        *got, self.token = pl.pallas_call(
            kernel,
            in_specs=[vmem] * count + [pl.BlockSpec(memory_space=pl.ANY)] * len(token),
            out_specs=[vmem] * (len(outs) + 1),
            out_shape=[jax.ShapeDtypeStruct(o, F32) for o in outs]
            + [jax.ShapeDtypeStruct((8, 128), F32)],
            scratch_shapes=list(scratch),
            compiler_params=pltpu.CompilerParams(vmem_limit_bytes=VMEM_LIMIT),
            cost_estimate=costs(cost),
            name=name,
        )(*ins, *token)
        return got


def load(partials):
    def body(source, target, sem):
        copy = pltpu.make_async_copy(source, target, sem)
        copy.start()
        copy.wait()

    return pl.pallas_call(
        body,
        in_specs=[pl.BlockSpec(memory_space=pltpu.HBM)],
        out_specs=pl.BlockSpec(memory_space=pltpu.VMEM),
        out_shape=jax.ShapeDtypeStruct(partials.shape, partials.dtype),
        scratch_shapes=[pltpu.SemaphoreType.DMA],
        compiler_params=pltpu.CompilerParams(vmem_limit_bytes=VMEM_LIMIT),
        cost_estimate=pl.CostEstimate(flops=4 * 2**30, bytes_accessed=0, transcendentals=0),
        name="load",
    )(partials)


def first_product(table, partials, starts, pair, after=None):
    x0 = 2 * pair

    def body(tab, p_low, p_high, x_ref, *rest):
        a_ref, bs_ref, bk_ref, cs_ref, ck_ref, left = rest[-6:]

        @pl.when(pl.program_id(1) == 0)
        def _():
            left[...] = split3(x_ref[0])

        for half, p_ref in enumerate((p_low, p_high)):
            for ey in range(4):
                rows = pl.ds(pl.multiple_of(tab[8 + ey] * 256, 256), 256)
                got = fold3(
                    lax.dot_general(
                        left[...],
                        p_ref[0, rows, :],
                        (((1,), (1,)), ((), ())),
                        preferred_element_type=F32,
                    )
                )
                a, b, c = (got[o : o + w] for o, w in zip(OFFSETS, WIDTHS))
                a_ref[0, ey, half, 0] = a
                (bk_ref if ey < 2 else bs_ref)[ey % 2, half, 0, 0] = b
                (cs_ref if half else ck_ref)[0, 0, ey] = c

    wa, wb, wc = WIDTHS
    shapes = [(2, 4, 2, 2, wa, 256)] + [(2, 2, 2, 2, wb, 256)] * 2 + [(2, 2, 4, wc, 256)] * 2
    blocks = [(1, 4, 2, 1, wa, 256)] + [(2, 2, 1, 1, wb, 256)] * 2 + [(1, 1, 4, wc, 256)] * 2
    maps = [
        lambda i, k, tab: (i, 0, 0, k, 0, 0),
        lambda i, k, tab: (0, 0, k, i, 0, 0),
        lambda i, k, tab: (0, 0, k, i, 0, 0),
        lambda i, k, tab: (k, i, 0, 0, 0),
        lambda i, k, tab: (k, i, 0, 0, 0),
    ]
    a, bs, bk, cs, ck = pl.pallas_call(
        body,
        grid_spec=pltpu.PrefetchScalarGridSpec(
            num_scalar_prefetch=1,
            grid=(2, 2),
            in_specs=[
                pl.BlockSpec((1, 1024, 512), lambda i, k, tab: (tab[i + x0], tab[4 + k], 0)),
                pl.BlockSpec((1, 1024, 512), lambda i, k, tab: (tab[i + x0], tab[6 + k], 0)),
                pl.BlockSpec((1, RANK, 512), lambda i, k, tab: (i, 0, 0)),
            ]
            + [pl.BlockSpec(memory_space=pl.ANY)] * (after is not None),
            out_specs=[pl.BlockSpec(b, m) for b, m in zip(blocks, maps)],
            scratch_shapes=[pltpu.VMEM((3 * RANK, 512), jnp.bfloat16)],
        ),
        out_shape=[jax.ShapeDtypeStruct(n, F32) for n in shapes],
        compiler_params=pltpu.CompilerParams(vmem_limit_bytes=VMEM_LIMIT),
        cost_estimate=pl.CostEstimate(
            flops=12 * 2**30, bytes_accessed=2**24, transcendentals=0
        ),
        name="first_product",
    )(table, partials, partials, starts, *([] if after is None else [after]))
    b_shape = (2, 4, 2, wb, 256)
    return (
        a.reshape(2, 4, 4, wa, 256),
        (bs.reshape(b_shape), bk.reshape(b_shape)),
        (cs, ck),
    )


def second_product(chain, pieces, table, partials, before=None, last=False):
    every = range(4)
    count = 2 + len(pieces) + (before is not None)

    def body(tab, p_ref, *refs):
        images = refs[: len(pieces)]
        outs = refs[count - 1 :]
        total = outs[-1]
        outs[0][...] = jnp.zeros((8, 128), F32)
        if before is None:
            total[...] = jnp.zeros((4, RANK, 512), F32)
        else:
            total[...] = refs[len(pieces)][...]

        def cell(x, z, y):
            row = pl.multiple_of(tab[4 + z] * 1024 + tab[8 + y] * 256, 256)
            return p_ref[tab[x], pl.ds(row, 256), :]

        def add(x, part, terms):
            got = None
            for v, p in terms:
                term = jnp.dot(split3(v), p, preferred_element_type=F32)
                got = term if got is None else got + term
            rows = slice(OFFSETS[part], OFFSETS[part] + WIDTHS[part])
            total[x, rows, :] += fold3(got)

        for (part, (half, start, size, low), _), v in zip(pieces, images):
            first = 2 * half

            @pl.loop(0, v.shape[2] if part == 1 else 2 if part == 0 else size)
            def _(n, part=part, first=first, start=start, size=size, low=low, v=v):
                if part == 0:
                    x = first + n
                    cells = [(v[n, k, z], (x, z, start + k)) for k in range(size) for z in every]
                elif part == 1:
                    x = low + n
                    cells = [
                        (v[j, k, n], (x, start + k, first + j)) for j in range(2) for k in range(size)
                    ]
                else:
                    x = start + n
                    cells = [(v[j, n, y], (x, first + j, y)) for j in range(2) for y in every]
                add(x, part, [(rows, cell(*c)) for rows, c in cells])

        if last:
            first = tab[12] == 0
            for x in every:
                left, right = total[x, :, :256], total[x, :, 256:]
                outs[2][x] = jnp.where(first, left, right)
                outs[3][(0, 2, 1, 3)[x]] = jnp.where(first, right, left)

    vmem = pl.BlockSpec(memory_space=pltpu.VMEM)
    operands = [partials] + [rows for _, _, rows in pieces]
    operands += ([] if before is None else [before]) + [chain.token]
    shapes = [(4, RANK, 256)] * 2 if last else [(4, RANK, 512)]
    chain.token, partials, *got = pl.pallas_call(
        body,
        in_specs=[pl.BlockSpec(memory_space=pltpu.SMEM)]
        + [vmem] * (len(operands) - 1)
        + [pl.BlockSpec(memory_space=pl.ANY)],
        out_specs=[vmem] * (2 + len(shapes)),
        out_shape=[
            jax.ShapeDtypeStruct((8, 128), F32),
            jax.ShapeDtypeStruct(partials.shape, partials.dtype),
        ]
        + [jax.ShapeDtypeStruct(n, F32) for n in shapes],
        scratch_shapes=[pltpu.VMEM((4, RANK, 512), F32)] if last else [],
        input_output_aliases={1: 1},
        compiler_params=pltpu.CompilerParams(vmem_limit_bytes=VMEM_LIMIT),
        cost_estimate=costs(0),
        name="second_product",
    )(table, *operands)
    return partials, got


def at_half(axis, half):
    index = [slice(None)] * 5
    index[axis] = slice(2 * half, 2 * half + 2)
    return tuple(index)


def add_all(chain, jobs, cost=1):
    outs = []
    for keep, _, axis in jobs:
        shape = list(keep.shape)
        if axis is not None:
            shape[axis] = 2
        outs += [tuple(shape)] * (1 if axis is None else 2)

    def body(*refs):
        n = 2 * len(jobs)
        for j, (_, _, axis) in enumerate(jobs):
            k_ref, g_ref = refs[2 * j], refs[2 * j + 1]
            if axis is None:
                refs[n][...] = k_ref[...] + g_ref[...]
                n += 1
            else:
                for half, out in ((1, refs[n]), (0, refs[n + 1])):
                    out[...] = k_ref[at_half(axis, half)] + g_ref[at_half(axis, half)]
                n += 2

    return chain.call("add_all", body, [v for k, g, _ in jobs for v in (k, g)], outs, (), cost)


def add_whole(chain, keep, got):
    return add_all(chain, [(keep, got, None)])[0]


def add_four(chain, keep, gots):
    def body(k_ref, a_ref, b_ref, c_ref, out):
        out[...] = (k_ref[...] + a_ref[...]) + (b_ref[...] + c_ref[...])

    return chain.call("add_four", body, [keep, *gots], [keep.shape])[0]


def add_flipped(chain, keeps, gots, axis):
    def body(*refs):
        for k_ref, g_ref, out in zip(refs[:3], refs[3:6], refs[6:]):
            for n in range(2):
                at = [slice(None)] * 5
                to = [slice(None)] * 5
                at[axis], to[axis] = slice(1 - n, 2 - n), slice(n, n + 1)
                out[tuple(to)] = k_ref[tuple(to)] + g_ref[tuple(at)]

    return chain.call("add_flipped", body, [*keeps, *gots], [v.shape for v in keeps])


def join(chain, pairs, axis):
    outs = []
    for pair in pairs:
        shape = list(pair[0].shape)
        shape[axis] *= len(pair)
        outs.append(tuple(shape))

    def body(*refs):
        n = 0
        for pair, out in zip(pairs, refs[-len(pairs) :]):
            if len(pair) == 1:
                out[...] = refs[n][...]
            else:
                for half in range(2):
                    out[at_half(axis, half)] = refs[n + half][...]
            n += len(pair)

    return chain.call("join", body, [v for pair in pairs for v in pair], outs)


def regroup(chain, held, beside):
    (a, b, _), (a_high, b_high, c_high) = held, beside
    shape = (2, 4, 2) + b.shape[3:]

    def body(a_low, a_up, b_low, b_up, c_ref, a_out, b_first, b_second, c_out):
        for half, (a_ref, b_ref) in enumerate(((a_low, b_low), (a_up, b_up))):
            a_out[at_half(1, half)] = a_ref[...]
            b_first[at_half(1, half)] = b_ref[at_half(2, 0)]
            b_second[at_half(1, half)] = b_ref[at_half(2, 1)]
        c_out[...] = c_ref[...]

    ins = [a, a_high, b, b_high, c_high]
    outs = [(2, 4) + a.shape[2:], shape, shape, c_high.shape]
    return chain.call("regroup", body, ins, outs)


def image_sum(chain, first, second):
    (a0, b0, c0), (a1, b1, c1) = first, second
    got_b0, got_c0 = hop(b0[0], "y", 0), hop(c0[0], "z", 0)
    got_b1, got_c1, got_a = hop(b1[0], "y", 0), hop(c1[0], "z", 0), hop(a1, "x", 0)
    up_b0, low_b0, low_c = add_all(chain, [(b0[1], got_b0, 1), (c0[1], got_c0, None)], 16)
    up_b1, low_b1, up_c, up_a, low_a = add_all(
        chain, [(b1[1], got_b1, 1), (c1[1], got_c1, None), (a0, got_a, 1)]
    )
    got_b0, got_b1 = hop(up_b0, "z", 0), hop(up_b1, "z", 0)
    got_c, got_a = hop(up_c, "x", 0), hop(up_a, "y", 0)
    low_b, up_b, up_c, low_c, up_a, low_a = add_all(
        chain, [(low_b0, got_b0, None), (low_b1, got_b1, None), (low_c, got_c, 2), (low_a, got_a, 2)]
    )
    keeps = [low_a, low_b, low_c]
    gots = [hop(up_a, "z", 0), hop(up_b, "x", 0), hop(up_c, "y", 0)]
    sums = add_all(chain, [(k, g, None) for k, g in zip(keeps, gots)])
    for axis in range(3):
        gots = [hop(v, o[axis], 1) for v, o in zip(sums, ORDERS)]
        sums = add_flipped(chain, sums, gots, axis)
    return sums


def gram_of(chain, blocks, images, before=None):
    arrays = [v for image in images for v in image]

    def body(*refs):
        out, image = refs[-2:]
        total = None if before is None else refs[len(arrays)][...]
        for z, y in blocks:
            pos = {"x": 0, "y": y, "z": z}
            for p in range(3):
                first, second, third = (pos[ax] for ax in ORDERS[p])
                ref = refs[3 * (2 * (first // 2) + second // 2) + p]
                rows = slice(OFFSETS[p], OFFSETS[p] + WIDTHS[p])
                image[rows, :] = ref[first % 2, second % ref.shape[1], third]
            got = precise_dot(image[...], image[...], ((1,), (1,))) / ORDER
            total = got if total is None else total + got
        out[...] = total

    return chain.call(
        "gram_of",
        body,
        arrays + ([] if before is None else [before]),
        [(RANK, RANK)],
        [pltpu.VMEM((RANK, RANK), F32)],
    )[0]


def normal_gram(chain, inverse, product):
    def body(i_ref, p_ref, image, gram):
        image[...] = precise_dot(i_ref[...], p_ref[...], ((1,), (0,)))
        gram[...] = precise_dot(image[...], image[...], ((1,), (1,))) / ORDER

    return chain.call(
        "normal_gram", body, [inverse, product], [(RANK, RANK)] * 2
    )


def sum_gram(chain, gram):
    core = lax.axis_index("row")
    half = RANK // 2
    mine = lax.dynamic_slice_in_dim(gram, core * half, half, 0)
    other = lax.dynamic_slice_in_dim(gram, (1 - core) * half, half, 0)
    mine = add_whole(chain, mine, swap_core(other))
    for axis in "yz":
        mine = add_four(chain, mine, [hop(mine, axis, step) for step in range(3)])
    other = swap_core(mine)
    low = jnp.where(core == 0, mine, other)
    high = jnp.where(core == 0, other, mine)
    return jnp.concatenate([low, high], axis=0)


BLOCK = 64


def block_inverse(block):
    row = lax.broadcasted_iota(jnp.int32, (BLOCK, 128), 0)
    col = lax.broadcasted_iota(jnp.int32, (BLOCK, 128), 1)
    both = jnp.concatenate([block, jnp.zeros((BLOCK, 128 - BLOCK), F32)], axis=1)
    both = jnp.where(col == row + BLOCK, 1.0, both)
    for s in range(0, BLOCK, 8):
        cols = [jnp.broadcast_to(both[:, s + j : s + j + 1], (BLOCK, 128)) for j in range(8)]
        for k in range(8):
            at = s + k
            scale = lax.rsqrt(jnp.broadcast_to(cols[k][at : at + 1, :], (8, 128)))[:1]
            pivot = both[at : at + 1, :] * scale
            below = jnp.where(row > at, cols[k] * scale, 0.0)
            for j in range(k + 1, 8):
                cols[j] = cols[j] - below * (cols[j][at : at + 1, :] * scale)
            both = jnp.where(row == at, pivot, both - below * pivot)
    return both[:, BLOCK:]


def eliminate(gram, inverse, work):
    row = lax.broadcasted_iota(jnp.int32, (RANK, RANK), 0)
    col = lax.broadcasted_iota(jnp.int32, (RANK, RANK), 1)
    work[:, :RANK] = gram[...]
    work[:, RANK:] = (row == col).astype(F32)
    for at in range(0, RANK, BLOCK):
        rows = slice(at, at + BLOCK)
        low = at // 128 * 128
        high = RANK + (at + BLOCK + 127) // 128 * 128
        upper = precise_dot(block_inverse(work[rows, rows]), work[rows, low:high], ((1,), (0,)))
        inverse[rows, : high - RANK] = upper[:, RANK - low :]
        if high < 2 * RANK:
            inverse[rows, high - RANK :] = jnp.zeros((BLOCK, 2 * RANK - high), F32)
        if at + BLOCK < RANK:
            left = upper[:, at + BLOCK - low : RANK - low]
            work[at + BLOCK :, low:high] -= precise_dot(left, upper, ((0,), (0,)))


def lower_inverse(chain, gram):
    return chain.call(
        "lower_inverse",
        eliminate,
        [gram],
        [(RANK, RANK)],
        [pltpu.VMEM((RANK, 2 * RANK), F32)],
    )[0]


def normalise(chain, gram, image):
    def body(g_ref, i_ref, out, inverse, work):
        eliminate(g_ref, inverse, work)
        out[0] = precise_dot(i_ref[...], inverse[...], ((0,), (1,)))

    return chain.call(
        "normalise",
        body,
        [gram, image],
        [(1, 256, RANK)],
        [pltpu.VMEM((RANK, RANK), F32), pltpu.VMEM((RANK, 2 * RANK), F32)],
    )[0]


def on_device(partials, slot_factor, previous):
    partials = load(partials[0])
    core = lax.axis_index("row")
    grp = lax.axis_index("grp")
    col = lax.axis_index("col")
    masks = jnp.where(
        core == 0, jnp.array([0, 3, 1, 2], jnp.int32), jnp.array([0, 1, 3, 2], jnp.int32)
    )
    table = jnp.concatenate(
        [
            slot_factor[grp ^ masks],
            (col // 4) ^ masks,
            (col % 4) ^ masks,
            jnp.stack([core, 1 - core]).astype(jnp.int32),
        ]
    )
    start = previous[0].T
    pair = jnp.stack([start, hop(start, "x", 1)])
    other = hop(pair, "x", 0)

    chain = Chain()
    first = first_product(table, partials, pair, 0)
    second = first_product(table, partials, other, 1, first[0])
    held = image_sum(chain, first, second)

    gots = [hop(v, o[2], 0) for v, o in zip(held, ORDERS)]
    low, high = (0, 1), (2, 3)
    gram = gram_of(chain, [(z, y) for z in low for y in low], [held])
    held = join(chain, list(zip(held, gots)), 2)
    beside = [hop(v, o[1], 0) for v, o in zip(held, ORDERS)]
    far_c = hop(held[2], "z", 0)

    product = functools.partial(second_product, chain, table=table)
    pieces = [(p, (0, 0, 2, 0), held[p]) for p in range(3)]
    partials, total = product(pieces, partials=partials)
    whole_a, first_b, second_b, beside_c = regroup(chain, held, beside)
    far_b = hop(first_b, "y", 0)
    far_a = hop(whole_a, "x", 0)
    last_b, last_c = hop(second_b, "y", 0), hop(beside_c, "z", 0)
    pieces = [(p, (0, 2, 2, 0), v) for p, v in enumerate([beside[0], beside[1], beside_c])]
    partials, total = product(pieces, partials=partials, before=total[0])
    blocks = [(z, y) for z in range(4) for y in range(4) if z > 1 or y > 1]
    images = [
        [held[0], held[1], held[2]],
        [beside[0], beside[1], held[2]],
        [held[0], far_b, far_c],
        [held[0], far_b, far_c],
    ]
    gram = gram_of(chain, blocks, images, gram)
    other = swap_core(gram)
    pieces = [(1, (1, 0, 4, 0), far_b), (2, (1, 0, 2, 0), far_c)]
    partials, total = product(pieces, partials=partials, before=total[0])
    inverse = lower_inverse(chain, add_whole(chain, gram, other))
    pieces = [(0, (1, 0, 4, 0), far_a), (1, (1, 0, 4, 2), last_b), (2, (1, 2, 2, 0), last_c)]
    _, (mine, other_mine) = product(pieces, partials=partials, before=total[0], last=True)
    mine = mine + swap_core(other_mine)
    mine = mine[:2] + hop(mine[2:], "x", 0)
    product = mine[0] + hop(mine[1], "x", 1)

    image, gram = normal_gram(chain, inverse, product)
    return normalise(chain, sum_gram(chain, gram), image)


def solution(mesh):
    return jax.shard_map(
        on_device,
        mesh=mesh,
        in_specs=(P("grp", None, "row", "col"), P(), P("grp", "col", None)),
        out_specs=P("grp", ("col", "row"), None),
        check_vma=False,
    )
```

```python
import functools

import jax
import jax.numpy as jnp
from jax import lax
from jax.experimental import pallas as pl
from jax.experimental.pallas import tpu as pltpu
from jax.sharding import PartitionSpec as P

ORDER = 8192
RANK = 256
PRECISE = lax.Precision.HIGHEST
NAMES = ("grp", "row", "col")
F32 = jnp.float32
VMEM_LIMIT = 16 * 2**20


def costs(size):
    return pl.CostEstimate(flops=size * 2**30, bytes_accessed=0, transcendentals=0)

MASKS = ((1, 3, 2), (3, 1, 2))
ORDERS = ("xyz", "yzx", "zxy")
WIDTHS = (64, 96, 96)
OFFSETS = (0, 64, 160)


def hop(value, axis, step):
    pairs = []
    for g in range(4):
        for r in range(2):
            mask = MASKS[r][step]
            for z in range(4):
                for y in range(4):
                    gg = g ^ mask if axis == "x" else g
                    zz = z ^ mask if axis == "z" else z
                    yy = y ^ mask if axis == "y" else y
                    pairs.append(((g * 2 + r) * 16 + z * 4 + y, (gg * 2 + r) * 16 + zz * 4 + yy))
    return lax.ppermute(value, NAMES, pairs)


def swap_core(value):
    return lax.ppermute(value, "row", [(0, 1), (1, 0)])


def precise_dot(left, right, dims):
    return lax.dot_general(
        left, right, (dims, ((), ())), precision=PRECISE, preferred_element_type=F32
    )


def split3(value):
    high = value.astype(jnp.bfloat16)
    rest = value - high.astype(F32)
    mid = rest.astype(jnp.bfloat16)
    low = (rest - mid.astype(F32)).astype(jnp.bfloat16)
    return jnp.concatenate([high, mid, low], axis=0)


def fold3(product):
    n = product.shape[0] // 3
    return product[:n] + (product[n : 2 * n] + product[2 * n :])


class Chain:
    def __init__(self):
        self.token = None

    def call(self, name, body, ins, outs, scratch=(), cost=1):
        token = [] if self.token is None else [self.token]
        count = len(ins)

        def kernel(*refs):
            mine = refs[:count] + refs[count + len(token) :]
            mine = mine[: count + len(outs)] + mine[count + len(outs) + 1 :]
            refs[count + len(token) + len(outs)][...] = jnp.zeros((8, 128), F32)
            body(*mine)

        vmem = pl.BlockSpec(memory_space=pltpu.VMEM)
        *got, self.token = pl.pallas_call(
            kernel,
            in_specs=[vmem] * count + [pl.BlockSpec(memory_space=pl.ANY)] * len(token),
            out_specs=[vmem] * (len(outs) + 1),
            out_shape=[jax.ShapeDtypeStruct(o, F32) for o in outs]
            + [jax.ShapeDtypeStruct((8, 128), F32)],
            scratch_shapes=list(scratch),
            compiler_params=pltpu.CompilerParams(vmem_limit_bytes=VMEM_LIMIT),
            cost_estimate=costs(cost),
            name=name,
        )(*ins, *token)
        return got


def load(partials):
    def body(source, target, sem):
        copy = pltpu.make_async_copy(source, target, sem)
        copy.start()
        copy.wait()

    return pl.pallas_call(
        body,
        in_specs=[pl.BlockSpec(memory_space=pltpu.HBM)],
        out_specs=pl.BlockSpec(memory_space=pltpu.VMEM),
        out_shape=jax.ShapeDtypeStruct(partials.shape, partials.dtype),
        scratch_shapes=[pltpu.SemaphoreType.DMA],
        compiler_params=pltpu.CompilerParams(vmem_limit_bytes=VMEM_LIMIT),
        cost_estimate=pl.CostEstimate(flops=4 * 2**30, bytes_accessed=0, transcendentals=0),
        name="load",
    )(partials)


def first_product(table, partials, starts, pair, after=None):
    x0 = 2 * pair

    def body(tab, p_low, p_high, x_ref, *rest):
        a_ref, bs_ref, bk_ref, cs_ref, ck_ref, left = rest[-6:]

        @pl.when(pl.program_id(1) == 0)
        def _():
            left[...] = split3(x_ref[0])

        for half, p_ref in enumerate((p_low, p_high)):
            for ey in range(4):
                rows = pl.ds(pl.multiple_of(tab[8 + ey] * 256, 256), 256)
                got = fold3(
                    lax.dot_general(
                        left[...],
                        p_ref[0, rows, :],
                        (((1,), (1,)), ((), ())),
                        preferred_element_type=F32,
                    )
                )
                a, b, c = (got[o : o + w] for o, w in zip(OFFSETS, WIDTHS))
                a_ref[0, ey, half, 0] = a
                (bk_ref if ey < 2 else bs_ref)[ey % 2, half, 0, 0] = b
                (cs_ref if half else ck_ref)[0, 0, ey] = c

    wa, wb, wc = WIDTHS
    shapes = [(2, 4, 2, 2, wa, 256)] + [(2, 2, 2, 2, wb, 256)] * 2 + [(2, 2, 4, wc, 256)] * 2
    blocks = [(1, 4, 2, 1, wa, 256)] + [(2, 2, 1, 1, wb, 256)] * 2 + [(1, 1, 4, wc, 256)] * 2
    maps = [
        lambda i, k, tab: (i, 0, 0, k, 0, 0),
        lambda i, k, tab: (0, 0, k, i, 0, 0),
        lambda i, k, tab: (0, 0, k, i, 0, 0),
        lambda i, k, tab: (k, i, 0, 0, 0),
        lambda i, k, tab: (k, i, 0, 0, 0),
    ]
    a, bs, bk, cs, ck = pl.pallas_call(
        body,
        grid_spec=pltpu.PrefetchScalarGridSpec(
            num_scalar_prefetch=1,
            grid=(2, 2),
            in_specs=[
                pl.BlockSpec((1, 1024, 512), lambda i, k, tab: (tab[i + x0], tab[4 + k], 0)),
                pl.BlockSpec((1, 1024, 512), lambda i, k, tab: (tab[i + x0], tab[6 + k], 0)),
                pl.BlockSpec((1, RANK, 512), lambda i, k, tab: (i, 0, 0)),
            ]
            + [pl.BlockSpec(memory_space=pl.ANY)] * (after is not None),
            out_specs=[pl.BlockSpec(b, m) for b, m in zip(blocks, maps)],
            scratch_shapes=[pltpu.VMEM((3 * RANK, 512), jnp.bfloat16)],
        ),
        out_shape=[jax.ShapeDtypeStruct(n, F32) for n in shapes],
        compiler_params=pltpu.CompilerParams(vmem_limit_bytes=VMEM_LIMIT),
        cost_estimate=pl.CostEstimate(
            flops=12 * 2**30, bytes_accessed=2**24, transcendentals=0
        ),
        name="first_product",
    )(table, partials, partials, starts, *([] if after is None else [after]))
    b_shape = (2, 4, 2, wb, 256)
    return (
        a.reshape(2, 4, 4, wa, 256),
        (bs.reshape(b_shape), bk.reshape(b_shape)),
        (cs, ck),
    )


def second_product(chain, pieces, table, partials, before=None, last=False):
    every = range(4)
    count = 2 + len(pieces) + (before is not None)

    def body(tab, p_ref, *refs):
        images = refs[: len(pieces)]
        outs = refs[count - 1 :]
        total = outs[-1]
        outs[0][...] = jnp.zeros((8, 128), F32)
        if before is None:
            total[...] = jnp.zeros((4, RANK, 512), F32)
        else:
            total[...] = refs[len(pieces)][...]

        def cell(x, z, y):
            row = pl.multiple_of(tab[4 + z] * 1024 + tab[8 + y] * 256, 256)
            return p_ref[tab[x], pl.ds(row, 256), :]

        def add(x, part, terms):
            got = None
            for v, p in terms:
                term = jnp.dot(split3(v), p, preferred_element_type=F32)
                got = term if got is None else got + term
            rows = slice(OFFSETS[part], OFFSETS[part] + WIDTHS[part])
            total[x, rows, :] += fold3(got)

        for (part, (half, start, size, low), _), v in zip(pieces, images):
            first = 2 * half

            @pl.loop(0, v.shape[2] if part == 1 else 2 if part == 0 else size)
            def _(n, part=part, first=first, start=start, size=size, low=low, v=v):
                if part == 0:
                    x = first + n
                    cells = [(v[n, k, z], (x, z, start + k)) for k in range(size) for z in every]
                elif part == 1:
                    x = low + n
                    cells = [
                        (v[j, k, n], (x, start + k, first + j)) for j in range(2) for k in range(size)
                    ]
                else:
                    x = start + n
                    cells = [(v[j, n, y], (x, first + j, y)) for j in range(2) for y in every]
                add(x, part, [(rows, cell(*c)) for rows, c in cells])

        if last:
            first = tab[12] == 0
            for x in every:
                left, right = total[x, :, :256], total[x, :, 256:]
                outs[2][x] = jnp.where(first, left, right)
                outs[3][(0, 2, 1, 3)[x]] = jnp.where(first, right, left)

    vmem = pl.BlockSpec(memory_space=pltpu.VMEM)
    operands = [partials] + [rows for _, _, rows in pieces]
    operands += ([] if before is None else [before]) + [chain.token]
    shapes = [(4, RANK, 256)] * 2 if last else [(4, RANK, 512)]
    chain.token, partials, *got = pl.pallas_call(
        body,
        in_specs=[pl.BlockSpec(memory_space=pltpu.SMEM)]
        + [vmem] * (len(operands) - 1)
        + [pl.BlockSpec(memory_space=pl.ANY)],
        out_specs=[vmem] * (2 + len(shapes)),
        out_shape=[
            jax.ShapeDtypeStruct((8, 128), F32),
            jax.ShapeDtypeStruct(partials.shape, partials.dtype),
        ]
        + [jax.ShapeDtypeStruct(n, F32) for n in shapes],
        scratch_shapes=[pltpu.VMEM((4, RANK, 512), F32)] if last else [],
        input_output_aliases={1: 1},
        compiler_params=pltpu.CompilerParams(vmem_limit_bytes=VMEM_LIMIT),
        cost_estimate=costs(0),
        name="second_product",
    )(table, *operands)
    return partials, got


def at_half(axis, half):
    index = [slice(None)] * 5
    index[axis] = slice(2 * half, 2 * half + 2)
    return tuple(index)


def add_all(chain, jobs, cost=1):
    outs = []
    for keep, _, axis in jobs:
        shape = list(keep.shape)
        if axis is not None:
            shape[axis] = 2
        outs += [tuple(shape)] * (1 if axis is None else 2)

    def body(*refs):
        n = 2 * len(jobs)
        for j, (_, _, axis) in enumerate(jobs):
            k_ref, g_ref = refs[2 * j], refs[2 * j + 1]
            if axis is None:
                refs[n][...] = k_ref[...] + g_ref[...]
                n += 1
            else:
                for half, out in ((1, refs[n]), (0, refs[n + 1])):
                    out[...] = k_ref[at_half(axis, half)] + g_ref[at_half(axis, half)]
                n += 2

    return chain.call("add_all", body, [v for k, g, _ in jobs for v in (k, g)], outs, (), cost)


def add_whole(chain, keep, got):
    return add_all(chain, [(keep, got, None)])[0]


def add_four(chain, keep, gots):
    def body(k_ref, a_ref, b_ref, c_ref, out):
        out[...] = (k_ref[...] + a_ref[...]) + (b_ref[...] + c_ref[...])

    return chain.call("add_four", body, [keep, *gots], [keep.shape])[0]


def add_flipped(chain, keeps, gots, axis):
    def body(*refs):
        for k_ref, g_ref, out in zip(refs[:3], refs[3:6], refs[6:]):
            for n in range(2):
                at = [slice(None)] * 5
                to = [slice(None)] * 5
                at[axis], to[axis] = slice(1 - n, 2 - n), slice(n, n + 1)
                out[tuple(to)] = k_ref[tuple(to)] + g_ref[tuple(at)]

    return chain.call("add_flipped", body, [*keeps, *gots], [v.shape for v in keeps])


def join(chain, pairs, axis):
    outs = []
    for pair in pairs:
        shape = list(pair[0].shape)
        shape[axis] *= len(pair)
        outs.append(tuple(shape))

    def body(*refs):
        n = 0
        for pair, out in zip(pairs, refs[-len(pairs) :]):
            if len(pair) == 1:
                out[...] = refs[n][...]
            else:
                for half in range(2):
                    out[at_half(axis, half)] = refs[n + half][...]
            n += len(pair)

    return chain.call("join", body, [v for pair in pairs for v in pair], outs)


def regroup(chain, held, beside):
    (a, b, _), (a_high, b_high, c_high) = held, beside
    shape = (2, 4, 2) + b.shape[3:]

    def body(a_low, a_up, b_low, b_up, c_ref, a_out, b_first, b_second, c_out):
        for half, (a_ref, b_ref) in enumerate(((a_low, b_low), (a_up, b_up))):
            a_out[at_half(1, half)] = a_ref[...]
            b_first[at_half(1, half)] = b_ref[at_half(2, 0)]
            b_second[at_half(1, half)] = b_ref[at_half(2, 1)]
        c_out[...] = c_ref[...]

    ins = [a, a_high, b, b_high, c_high]
    outs = [(2, 4) + a.shape[2:], shape, shape, c_high.shape]
    return chain.call("regroup", body, ins, outs)


def add_halves(keep, got, axis, upper, lower):
    upper[...] = keep[at_half(axis, 1)] + got[at_half(axis, 1)]
    lower[...] = keep[at_half(axis, 0)] + got[at_half(axis, 0)]


def second_sums(chain, ins):
    def body(up0, kb, gb, kc, gc, ka, ga, up_b, low_b, up_c, up_a, low_a):
        up_b[at_half(2, 0)] = up0[...]
        up_b[at_half(2, 1)] = kb[at_half(1, 1)] + gb[at_half(1, 1)]
        low_b[...] = kb[at_half(1, 0)] + gb[at_half(1, 0)]
        up_c[...] = kc[...] + gc[...]
        add_halves(ka, ga, 1, up_a, low_a)

    wa, wb = WIDTHS[:2]
    a_shape, b_shape = (2, 2, 4, wa, 256), (2, 2, 4, wb, 256)
    outs = [b_shape, ins[0].shape, ins[3].shape, a_shape, a_shape]
    return chain.call("second_sums", body, ins, outs)


def third_sums(chain, ins):
    def body(b0, b1, gb, kc, gc, ka, ga, low_b, up_b, up_c, low_c, up_a, low_a):
        low_b[...] = b0[...] + gb[at_half(2, 0)]
        up_b[...] = b1[...] + gb[at_half(2, 1)]
        add_halves(kc, gc, 2, up_c, low_c)
        add_halves(ka, ga, 2, up_a, low_a)

    a_shape, b_shape, c_shape = ((2, 2, 2, w, 256) for w in WIDTHS)
    outs = [b_shape, b_shape, c_shape, c_shape, a_shape, a_shape]
    return chain.call("third_sums", body, ins, outs)


def image_sum(chain, first, second):
    (a0, b0, c0), (a1, b1, c1) = first, second
    got_b0, got_c0 = hop(b0[0], "y", 0), hop(c0[0], "z", 0)
    got_b1, got_c1, got_a = hop(b1[0], "y", 0), hop(c1[0], "z", 0), hop(a1, "x", 0)
    up_b0, low_b0, low_c = add_all(chain, [(b0[1], got_b0, 1), (c0[1], got_c0, None)], 16)
    up_b, low_b1, up_c, up_a, low_a = second_sums(
        chain, [up_b0, b1[1], got_b1, c1[1], got_c1, a0, got_a]
    )
    got_b, got_c, got_a = hop(up_b, "z", 0), hop(up_c, "x", 0), hop(up_a, "y", 0)
    low_b, up_b, up_c, low_c, up_a, low_a = third_sums(
        chain, [low_b0, low_b1, got_b, low_c, got_c, low_a, got_a]
    )
    keeps = [low_a, low_b, low_c]
    gots = [hop(up_a, "z", 0), hop(up_b, "x", 0), hop(up_c, "y", 0)]
    sums = add_all(chain, [(k, g, None) for k, g in zip(keeps, gots)])
    for axis in range(3):
        gots = [hop(v, o[axis], 1) for v, o in zip(sums, ORDERS)]
        sums = add_flipped(chain, sums, gots, axis)
    return sums


def gram_of(chain, blocks, images, before=None):
    arrays = [v for image in images for v in image]

    def body(*refs):
        out, image = refs[-2:]
        total = None if before is None else refs[len(arrays)][...]
        for z, y in blocks:
            pos = {"x": 0, "y": y, "z": z}
            for p in range(3):
                first, second, third = (pos[ax] for ax in ORDERS[p])
                ref = refs[3 * (2 * (first // 2) + second // 2) + p]
                rows = slice(OFFSETS[p], OFFSETS[p] + WIDTHS[p])
                image[rows, :] = ref[first % 2, second % ref.shape[1], third]
            got = precise_dot(image[...], image[...], ((1,), (1,))) / ORDER
            total = got if total is None else total + got
        out[...] = total

    return chain.call(
        "gram_of",
        body,
        arrays + ([] if before is None else [before]),
        [(RANK, RANK)],
        [pltpu.VMEM((RANK, RANK), F32)],
    )[0]


def normal_gram(chain, inverse, product):
    def body(i_ref, p_ref, image, gram):
        image[...] = precise_dot(i_ref[...], p_ref[...], ((1,), (0,)))
        gram[...] = precise_dot(image[...], image[...], ((1,), (1,))) / ORDER

    return chain.call(
        "normal_gram", body, [inverse, product], [(RANK, RANK)] * 2
    )


def sum_gram(chain, gram):
    core = lax.axis_index("row")
    half = RANK // 2
    mine = lax.dynamic_slice_in_dim(gram, core * half, half, 0)
    other = lax.dynamic_slice_in_dim(gram, (1 - core) * half, half, 0)
    mine = add_whole(chain, mine, swap_core(other))
    for axis in "yz":
        mine = add_four(chain, mine, [hop(mine, axis, step) for step in range(3)])
    other = swap_core(mine)
    low = jnp.where(core == 0, mine, other)
    high = jnp.where(core == 0, other, mine)
    return jnp.concatenate([low, high], axis=0)


BLOCK = 64


def block_inverse(block):
    row = lax.broadcasted_iota(jnp.int32, (BLOCK, 128), 0)
    col = lax.broadcasted_iota(jnp.int32, (BLOCK, 128), 1)
    both = jnp.concatenate([block, jnp.zeros((BLOCK, 128 - BLOCK), F32)], axis=1)
    both = jnp.where(col == row + BLOCK, 1.0, both)
    for s in range(0, BLOCK, 8):
        cols = [jnp.broadcast_to(both[:, s + j : s + j + 1], (BLOCK, 128)) for j in range(8)]
        for k in range(8):
            at = s + k
            scale = lax.rsqrt(jnp.broadcast_to(cols[k][at : at + 1, :], (8, 128)))[:1]
            pivot = both[at : at + 1, :] * scale
            below = jnp.where(row > at, cols[k] * scale, 0.0)
            for j in range(k + 1, 8):
                cols[j] = cols[j] - below * (cols[j][at : at + 1, :] * scale)
            both = jnp.where(row == at, pivot, both - below * pivot)
    return both[:, BLOCK:]


def eliminate(gram, inverse, work):
    row = lax.broadcasted_iota(jnp.int32, (RANK, RANK), 0)
    col = lax.broadcasted_iota(jnp.int32, (RANK, RANK), 1)
    work[:, :RANK] = gram[...]
    work[:, RANK:] = (row == col).astype(F32)
    for at in range(0, RANK, BLOCK):
        rows = slice(at, at + BLOCK)
        low = at // 128 * 128
        high = RANK + (at + BLOCK + 127) // 128 * 128
        upper = precise_dot(block_inverse(work[rows, rows]), work[rows, low:high], ((1,), (0,)))
        inverse[rows, : high - RANK] = upper[:, RANK - low :]
        if high < 2 * RANK:
            inverse[rows, high - RANK :] = jnp.zeros((BLOCK, 2 * RANK - high), F32)
        if at + BLOCK < RANK:
            left = upper[:, at + BLOCK - low : RANK - low]
            work[at + BLOCK :, low:high] -= precise_dot(left, upper, ((0,), (0,)))


def lower_inverse(chain, gram):
    return chain.call(
        "lower_inverse",
        eliminate,
        [gram],
        [(RANK, RANK)],
        [pltpu.VMEM((RANK, 2 * RANK), F32)],
    )[0]


def normalise(chain, gram, image):
    def body(g_ref, i_ref, out, inverse, work):
        eliminate(g_ref, inverse, work)
        out[0] = precise_dot(i_ref[...], inverse[...], ((0,), (1,)))

    return chain.call(
        "normalise",
        body,
        [gram, image],
        [(1, 256, RANK)],
        [pltpu.VMEM((RANK, RANK), F32), pltpu.VMEM((RANK, 2 * RANK), F32)],
    )[0]


def on_device(partials, slot_factor, previous):
    partials = load(partials[0])
    core = lax.axis_index("row")
    grp = lax.axis_index("grp")
    col = lax.axis_index("col")
    masks = jnp.where(
        core == 0, jnp.array([0, 3, 1, 2], jnp.int32), jnp.array([0, 1, 3, 2], jnp.int32)
    )
    table = jnp.concatenate(
        [
            slot_factor[grp ^ masks],
            (col // 4) ^ masks,
            (col % 4) ^ masks,
            jnp.stack([core, 1 - core]).astype(jnp.int32),
        ]
    )
    start = previous[0].T
    pair = jnp.stack([start, hop(start, "x", 1)])
    other = hop(pair, "x", 0)

    chain = Chain()
    first = first_product(table, partials, pair, 0)
    second = first_product(table, partials, other, 1, first[0])
    held = image_sum(chain, first, second)

    gots = [hop(v, o[2], 0) for v, o in zip(held, ORDERS)]
    low, high = (0, 1), (2, 3)
    gram = gram_of(chain, [(z, y) for z in low for y in low], [held])
    held = join(chain, list(zip(held, gots)), 2)
    beside = [hop(v, o[1], 0) for v, o in zip(held, ORDERS)]
    far_c = hop(held[2], "z", 0)

    product = functools.partial(second_product, chain, table=table)
    pieces = [(p, (0, 0, 2, 0), held[p]) for p in range(3)]
    partials, total = product(pieces, partials=partials)
    whole_a, first_b, second_b, beside_c = regroup(chain, held, beside)
    far_b = hop(first_b, "y", 0)
    far_a = hop(whole_a, "x", 0)
    last_b, last_c = hop(second_b, "y", 0), hop(beside_c, "z", 0)
    pieces = [(p, (0, 2, 2, 0), v) for p, v in enumerate([beside[0], beside[1], beside_c])]
    partials, total = product(pieces, partials=partials, before=total[0])
    blocks = [(z, y) for z in range(4) for y in range(4) if z > 1 or y > 1]
    images = [
        [held[0], held[1], held[2]],
        [beside[0], beside[1], held[2]],
        [held[0], far_b, far_c],
        [held[0], far_b, far_c],
    ]
    gram = gram_of(chain, blocks, images, gram)
    other = swap_core(gram)
    pieces = [(1, (1, 0, 4, 0), far_b), (2, (1, 0, 2, 0), far_c)]
    partials, total = product(pieces, partials=partials, before=total[0])
    inverse = lower_inverse(chain, add_whole(chain, gram, other))
    pieces = [(0, (1, 0, 4, 0), far_a), (1, (1, 0, 4, 2), last_b), (2, (1, 2, 2, 0), last_c)]
    _, (mine, other_mine) = product(pieces, partials=partials, before=total[0], last=True)
    mine = mine + swap_core(other_mine)
    mine = mine[:2] + hop(mine[2:], "x", 0)
    product = mine[0] + hop(mine[1], "x", 1)

    image, gram = normal_gram(chain, inverse, product)
    return normalise(chain, sum_gram(chain, gram), image)


def solution(mesh):
    return jax.shard_map(
        on_device,
        mesh=mesh,
        in_specs=(P("grp", None, "row", "col"), P(), P("grp", "col", None)),
        out_specs=P("grp", ("col", "row"), None),
        check_vma=False,
    )
```
